32 devices in a mesh: batch: 4 (over z), pencil: 8 (over y, x, core).
Axes of the slice: x: 2, y: 2, z: 4, core: 2. Of those that a mesh axis runs over, the one named last changes fastest.
Arguments:
- state_field: float32 [8, 128, 32, 32, 128], P('batch', 'pencil'), may hold values from -6 to 6
- spectral_weight: float32 [128, 2, 32, 32, 16], P('pencil'), may hold values from -6 to 6
- local_weight: float32 [32, 32], replicated, may hold values from -1 to 1
- channel_bias: float32 [32], replicated, may hold values from -3 to 3
- cotangent: float32 [8, 128, 32, 32, 128], P('batch', 'pencil'), may hold values from -6 to 6
Outputs:
- layer_out: float32 [8, 128, 32, 32, 128], P('batch', 'pencil')
- grad_state: float32 [8, 128, 32, 32, 128], P('batch', 'pencil')
- grad_spectral: float32 [128, 2, 32, 32, 16], P('pencil')
- grad_local: float32 [32, 32], replicated
- grad_bias: float32 [32], replicated
The draws below stay inside these ranges and needn't reach their ends.
All inputs are finite; a program needn't handle non-finite values.
Results may differ from the reference program's by a relative error of at most 0.00011.
Values sent between devices are 32-bit elements; how exact they have to be, the bound alone decides.
No kernel may reach another device: no remote copies, remote signals or barrier semaphores. Data moves between devices by JAX's collectives and lax.ppermute only.
A program may use at most 256 MiB of HBM per device.

```python
import math
import jax
import jax.numpy as jnp
from jax import lax

X = 128
Y = 128
Z = 32
C = 32
MX = 16
MY = 16
MZ = 8
SAMPLES = 8


def levels(stream_key, extent, pieces, smallest, top_value):
    loudness = 1.0
    for dim, shards_of in pieces:
        heights = jax.random.uniform(jax.random.fold_in(jax.random.fold_in(stream_key, 6), dim), (shards_of,), jnp.float32, smallest / len(pieces), top_value / len(pieces))
        loudness = loudness * jnp.repeat(jnp.exp(heights), extent[dim] // shards_of).reshape((-1,) + (1,) * (len(extent) - 1 - dim))
    return loudness


def scatter_about(key, shape, spread, bound, cuts=(), kind=jnp.bfloat16):
    values = jax.random.normal(key, shape, jnp.float32) * spread
    if len(cuts) > 0:
        values = levels(key, shape, cuts, -0.22, 0.18) * values
    return jnp.clip(values, min=-bound, max=bound).astype(kind)


def setup_inputs(seed: int = 0) -> dict:
    seeds = jax.random.split(jax.random.key(seed), 6)
    state_field = scatter_about(seeds[0], (SAMPLES, Y, C, Z, X), 1.0, 6.0, ((0, 4), (1, 8)), jnp.float32)
    spectral_weight = scatter_about(seeds[1], (MX * MZ, 2, C, C, MY), 1.1, 6.0, ((0, 8),), jnp.float32)
    local_weight = scatter_about(seeds[2], (C, C), C ** -0.5, 1.0, (), jnp.float32)
    channel_bias = scatter_about(seeds[3], (C,), 0.5, 3.0, (), jnp.float32)
    cotangent = scatter_about(seeds[4], (SAMPLES, Y, C, Z, X), 1.0, 6.0, ((0, 4), (1, 8)), jnp.float32)
    return {"state_field": state_field, "spectral_weight": spectral_weight, "local_weight": local_weight, "channel_bias": channel_bias, "cotangent": cotangent}


def contract(form, left, right):
    return jnp.einsum(form, left, right, precision=lax.Precision.HIGHEST)

def tables(points, kept_modes):
    position = jnp.arange(points, dtype=jnp.int32)
    mode_order = jnp.arange(kept_modes, dtype=jnp.int32)
    frequency = jnp.where(mode_order < kept_modes // 2, mode_order, points - kept_modes + mode_order)
    phases = position[:, None] * frequency[None, :] % points
    angles = phases.astype(jnp.float32) * (2.0 * math.pi / points)
    return (jnp.cos(angles), jnp.sin(angles))

def spectral_sample(sample, weight):
    cos_x, sin_x = tables(X, MX)
    cos_y, sin_y = tables(Y, MY)
    cos_z, sin_z = tables(Z, MZ)
    scaling = 1.0 / math.sqrt(X * Y * Z)
    x_real = contract('yczx,xk->yczk', sample, cos_x)
    x_imag = -contract('yczx,xk->yczk', sample, sin_x)
    z_real = contract('yczk,zj->kjcy', x_real, cos_z) + contract('yczk,zj->kjcy', x_imag, sin_z)
    z_imag = contract('yczk,zj->kjcy', x_imag, cos_z) - contract('yczk,zj->kjcy', x_real, sin_z)
    z_real = z_real.reshape(MX * MZ, C, Y) * scaling
    z_imag = z_imag.reshape(MX * MZ, C, Y) * scaling
    a_real = contract('mcy,yq->mcq', z_real, cos_y) + contract('mcy,yq->mcq', z_imag, sin_y)
    a_imag = contract('mcy,yq->mcq', z_imag, cos_y) - contract('mcy,yq->mcq', z_real, sin_y)
    w_real = weight[:, 0]
    w_imag = weight[:, 1]
    b_real = contract('miq,mioq->moq', a_real, w_real) - contract('miq,mioq->moq', a_imag, w_imag)
    b_imag = contract('miq,mioq->moq', a_real, w_imag) + contract('miq,mioq->moq', a_imag, w_real)
    y_real = contract('moq,yq->moy', b_real, cos_y) - contract('moq,yq->moy', b_imag, sin_y)
    y_imag = contract('moq,yq->moy', b_imag, cos_y) + contract('moq,yq->moy', b_real, sin_y)
    y_real = y_real.reshape(MX, MZ, C, Y)
    y_imag = y_imag.reshape(MX, MZ, C, Y)
    back_real = contract('kjoy,zj->yozk', y_real, cos_z) - contract('kjoy,zj->yozk', y_imag, sin_z)
    back_imag = contract('kjoy,zj->yozk', y_imag, cos_z) + contract('kjoy,zj->yozk', y_real, sin_z)
    return (contract('yozk,xk->yozx', back_real, cos_x) - contract('yozk,xk->yozx', back_imag, sin_x)) * scaling

def layer(sample, weight, local_weight, channel_bias):
    pre_act = spectral_sample(sample, weight) + contract('yczx,co->yozx', sample, local_weight) + channel_bias[None, :, None, None]
    return jax.nn.gelu(pre_act, approximate=True)

def reference(state_field, spectral_weight, local_weight, channel_bias, cotangent):

    def advance(carry, items):
        sample, grad_out = items
        result, pullback = jax.vjp(layer, sample, spectral_weight, local_weight, channel_bias)
        grad_sample, grad_weight, grad_lw, grad_cb = pullback(grad_out)
        return ((carry[0] + grad_weight, carry[1] + grad_lw, carry[2] + grad_cb), (result, grad_sample))
    start_carry = (jnp.zeros(spectral_weight.shape, jnp.float32), jnp.zeros(local_weight.shape, jnp.float32), jnp.zeros(channel_bias.shape, jnp.float32))
    totals, stacked = lax.scan(advance, start_carry, (state_field, cotangent))
    scaling = 1.0 / math.sqrt(SAMPLES * X * Y * Z)
    return (stacked[0], stacked[1], totals[0], totals[1] * scaling, totals[2] * scaling)
```

```python
import functools
import math

import jax
import jax.numpy as jnp
import ml_dtypes
import numpy as np
from jax import lax
from jax.experimental import pallas as pl
from jax.experimental.pallas import tpu as pltpu
from jax.sharding import PartitionSpec as P

X = 128
Y = 128
Z = 32
C = 32
MX = 16
MY = 16
MZ = 8
MODES = MX * MZ
CQ = C * MY
ZJ = 9
ZJP = 10
GX = 4 * X
YB = 4

F32 = jnp.float32
BF16 = jnp.bfloat16
gelu_scale = math.sqrt(2.0 / math.pi)
cubic_term = 0.044715
VMEM_LIMIT = 56 * 1024 * 1024


def np_split(a):
    a = np.asarray(a, np.float32)
    hi = a.astype(ml_dtypes.bfloat16)
    lo = (a - hi.astype(np.float32)).astype(ml_dtypes.bfloat16)
    return hi, lo


def freqs(kept):
    return np.array([j if j < kept // 2 else j - kept for j in range(kept)])


def z_functions():
    z = np.arange(Z)
    rows = [np.cos(2 * np.pi * (j * z % Z) / Z) for j in range(5)]
    rows += [np.sin(2 * np.pi * (j * z % Z) / Z) for j in range(1, 5)]
    rows += [np.ones(Z)]
    return np.stack(rows)


def z_forward_table():
    zt = z_functions().reshape(ZJP, 4, 8)
    t = np.einsum("jab,cd->jcadb", zt, np.eye(8)).reshape(ZJP * 8, 256)
    hi, lo = np_split(t)
    return np.concatenate([hi, lo], 0)


def z_inverse_table():
    zt = z_functions().reshape(ZJP, 4, 8)
    t = np.einsum("jab,cd->acbjd", zt, np.eye(8)).reshape(256, ZJP * 8)
    hi, lo = np_split(t)
    return np.concatenate([hi, hi, lo], 1)


def x_table():
    x = np.arange(X)
    t = np.zeros((2, MX, MZ, ZJ, X))
    for a, fx in enumerate(freqs(MX)):
        cx = np.cos(2 * np.pi * (fx * x % X) / X)
        sx = np.sin(2 * np.pi * (fx * x % X) / X)
        for b, fz in enumerate(freqs(MZ)):
            k = abs(fz)
            t[0, a, b, k] = cx
            t[1, a, b, k] = sx
            if k > 0:
                t[0, a, b, 4 + k] = -np.sign(fz) * sx
                t[1, a, b, 4 + k] = np.sign(fz) * cx
    t = t.reshape(2 * MODES, ZJ * X) / math.sqrt(X * Y * Z)
    hi, lo = np_split(t)
    return np.concatenate([hi, lo], 0)


def channel_group(yl):
    return min(C, max(8, X // yl))


def y_tables(yl):
    cg = channel_group(yl)
    f = freqs(MY)
    ang = 2 * np.pi * (np.arange(yl)[:, None] * f[None, :] % Y) / Y
    t = np.stack([np.cos(ang), np.sin(ang)])
    fwd = np.einsum("tyq,cd->yctdq", t, np.eye(cg)).reshape(yl * cg, 2 * cg * MY)
    inv = np.einsum("tyq,cd->dqtyc", t, np.eye(cg)).reshape(cg * MY, 2 * yl * cg)
    out = []
    for m in (fwd, inv):
        hi, lo = np_split(m)
        out.append(np.concatenate([hi, hi, lo], 0))
    return out


def cell_row(yl, y, g):
    cg = channel_group(yl)
    return (g * 8 // cg) * (yl * cg) + y * cg + g * 8 % cg


def phase_table(yl, pencils):
    f = freqs(MY)
    ang = 2 * np.pi * (np.arange(pencils)[:, None] * yl * f[None, :] % Y) / Y
    t = np.stack([np.cos(ang), np.sin(ang)], 1)
    t = np.tile(t, (1, 4, C))
    return t.astype(np.float32)


def split(v):
    hi = v.astype(BF16)
    lo = (v - hi.astype(F32)).astype(BF16)
    return hi, lo


def dot(a, b):
    return lax.dot_general(a, b, (((1,), (0,)), ((), ())), preferred_element_type=F32)


def dot_nt(a, b):
    return lax.dot_general(a, b, (((1,), (1,)), ((), ())), preferred_element_type=F32)


def dot3(a, bh, bl, f=dot):
    ah, al = split(a)
    return f(ah, bh) + f(al, bh) + f(ah, bl)


def iota(shape, dim):
    return lax.broadcasted_iota(jnp.int32, shape, dim)


def regroup(parts):
    return jnp.concatenate(
        [jnp.concatenate([p[g * 64 : (g + 1) * 64] for p in parts], 0) for g in range(4)], 1
    )


def load_parts(ref, y):
    return [ref[y, :, zo * 8 : (zo + 1) * 8, :].reshape(256, X) for zo in range(4)]


class Rows:
    def __init__(self, source, sample, held, sems):
        self.source, self.sample, self.held, self.sems = source, sample, held, sems
        self.blocks = sems.shape[0]
        self.deep = held.shape[0] // self.blocks

    def copy(self, block):
        rows = pl.ds(block * self.deep, self.deep)
        return pltpu.make_async_copy(
            self.source.at[self.sample, rows], self.held.at[rows], self.sems.at[block]
        )

    def start(self):
        for block in range(self.blocks):
            self.copy(block).start()


def z_forward(his, los, ltf_ref, rk, y):
    gh, gl = regroup(his), regroup(los)
    n = ZJP * 8
    yl = rk.shape[0] // C
    both = dot(ltf_ref[...], gh)
    r = both[:n] + both[n:] + dot(ltf_ref[:n, :], gl)
    for g in range(4):
        rows = pl.ds(pl.multiple_of(cell_row(yl, y, g), 8), 8)
        for j in range(ZJ):
            rk[rows, j * X : (j + 1) * X] = r[j * 8 : (j + 1) * 8, g * X : (g + 1) * X]
    return r[ZJ * 8 :]


def by_group(v, table_ref, group):
    rows, lanes = v.shape
    parts = lanes // group
    v = jnp.concatenate([v[:, k * group : (k + 1) * group] for k in range(parts)], 0)
    hi, lo = split(v)
    r = dot(jnp.concatenate([hi, lo], 1), table_ref[: 2 * group, :])
    r = r + dot(hi, table_ref[2 * group :, :])
    half = r.shape[1] // 2
    return [
        jnp.concatenate(
            [r[k * rows : (k + 1) * rows, t * half : (t + 1) * half] for k in range(parts)], 1
        )
        for t in range(2)
    ]


def to_modes(rk, xt_ref, yf_ref, ph_ref, out_ref):
    rh, rl = split(rk[...])
    both = dot_nt(xt_ref[...], rh)
    n = 2 * MODES
    ab = both[:n] + both[n:] + dot_nt(xt_ref[:n, :], rl)
    zc, zs = by_group(ab, yf_ref, yf_ref.shape[0] // 3)
    re = zc[:MODES] - zs[MODES:]
    im = -(zc[MODES:] + zs[:MODES])
    pc, ps = own_phase(ph_ref)
    groups = out_ref.shape[0]
    mg = MODES // groups
    out_ref[:, :mg, :] = (re * pc + im * ps).reshape(groups, mg, CQ)
    out_ref[:, mg : 2 * mg, :] = (im * pc - re * ps).reshape(groups, mg, CQ)


def from_modes(m_ref, xt_ref, yi_ref, ph_ref, bias_ref, qs):
    groups, rows, _ = m_ref.shape
    mg = rows // 2
    re0 = m_ref[:, :mg, :].reshape(MODES, CQ)
    im0 = m_ref[:, mg:, :].reshape(MODES, CQ)
    pc, ps = own_phase(ph_ref)
    m = jnp.concatenate([re0 * pc - im0 * ps, im0 * pc + re0 * ps], 0)
    zc, zs = by_group(m, yi_ref, yi_ref.shape[0] // 3)
    re = zc[:MODES] - zs[MODES:]
    im = zc[MODES:] + zs[:MODES]
    yt = jnp.concatenate([re, -im], 0).T
    q = dot3(yt, xt_ref[: 2 * MODES, :], xt_ref[2 * MODES :, :])
    n = ZJP * 8
    yl = qs.shape[0]
    for y in range(yl):
        pieces = []
        for j in range(ZJ):
            pieces.append(
                jnp.concatenate(
                    [
                        q[cell_row(yl, y, g) : cell_row(yl, y, g) + 8, j * X : (j + 1) * X]
                        for g in range(4)
                    ],
                    1,
                )
            )
        if bias_ref is None:
            pieces.append(jnp.zeros((8, GX), F32))
        else:
            pieces.append(bias_rows(bias_ref))
        hi, lo = split(jnp.concatenate(pieces, 0))
        qs[y, 0:n, :] = hi
        qs[y, n : 2 * n, :] = lo
        qs[y, 2 * n :, :] = hi


def weight_stack(w_ref, ws, f):
    spread = (iota((256, C), 0) // 8 == iota((256, C), 1)).astype(F32).astype(BF16)
    same = iota((256, 256), 0) % 8 == iota((256, 256), 1) % 8

    def wide(part):
        t = dot_nt(f(spread, part).astype(BF16), spread)
        return jnp.where(same, t, 0.0).astype(BF16)

    hi, lo = split(w_ref[...])
    ws[0:256, :] = wide(hi)
    ws[256:512, :] = wide(lo)


def pointwise(ws, xh, xl):
    both = dot(ws[...], xh)
    return both[:256] + both[256:] + dot(ws[0:256, :], xl)


def bias_rows(b_ref):
    diag = iota((C, C), 0) == iota((C, C), 1)
    col = jnp.sum(jnp.where(diag, b_ref[...], 0.0), axis=1, keepdims=True)
    return jnp.concatenate(
        [jnp.broadcast_to(col[g * 8 : (g + 1) * 8], (8, X)) for g in range(4)], 1
    )


def own_phase(ph_ref):
    own = ph_ref[lax.axis_index("pencil")]
    return own[0:1], own[1:2]


def forward_kernel(s, x_ref, ltf_ref, xt_ref, yf_ref, ph_ref, out_ref, rk, xs, x_sem):
    yb = pl.program_id(0)
    x = Rows(x_ref, s, xs, x_sem)
    deep = x.deep

    @pl.when(yb == 0)
    def _():
        x.start()

    x.copy(yb).wait()

    def step(y, carry):
        hl = [split(p) for p in load_parts(xs, yb * deep + y)]
        z_forward([h for h, _ in hl], [l for _, l in hl], ltf_ref, rk, yb * deep + y)
        return carry

    lax.fori_loop(0, deep, step, 0, unroll=True)

    @pl.when(yb == pl.num_programs(0) - 1)
    def _():
        to_modes(rk, xt_ref, yf_ref, ph_ref, out_ref)


def cell_kernel(
    s, x_ref, ct_ref, m_ref, w_ref, bias_ref, ltf_ref, lti_ref, xt_ref, yf_ref, yi_ref, ph_ref,
    *refs,
):
    out_ref, gp_ref, v_ref, rk, qs, ws, lacc, bacc, xs, x_sem, cts, ct_sem = refs[-12:]
    yb = pl.program_id(0)
    x = Rows(x_ref, s, xs, x_sem)
    ct = Rows(ct_ref, s, cts, ct_sem)
    deep = x.deep

    @pl.when(yb == 0)
    def _():
        x.start()
        ct.start()
        from_modes(m_ref, xt_ref, yi_ref, ph_ref, bias_ref, qs)
        weight_stack(w_ref, ws, dot_nt)
        lacc[...] = jnp.zeros_like(lacc)
        bacc[...] = jnp.zeros_like(bacc)

    x.copy(yb).wait()
    ct.copy(yb).wait()

    def step(y, carry):
        hl = [split(p) for p in load_parts(xs, yb * deep + y)]
        xh = jnp.concatenate([h for h, _ in hl], 1)
        xl = jnp.concatenate([l for _, l in hl], 1)
        conv = pointwise(ws, xh, xl)
        spec = dot(lti_ref[...], qs[yb * deep + y])
        ghs, gls = [], []
        for zo in range(4):
            gs = []
            for g in range(4):
                p = (
                    conv[g * 64 : (g + 1) * 64, zo * X : (zo + 1) * X]
                    + spec[zo * 64 : (zo + 1) * 64, g * X : (g + 1) * X]
                )
                p2 = p * p
                u = p2 * (gelu_scale * cubic_term) + gelu_scale
                t = jnp.tanh(p * u)
                h = 0.5 * t + 0.5
                o = p * h
                d = p2 * (1.5 * gelu_scale * cubic_term) + 0.5 * gelu_scale
                slope = h + p * (1.0 - t * t) * d
                where = (0, y, slice(g * 8, (g + 1) * 8), slice(zo * 8, (zo + 1) * 8))
                out_ref[where] = o.reshape(8, 8, X)
                gp = cts[(yb * deep + y,) + where[2:]].reshape(64, X) * slope
                gp_ref[where] = gp.reshape(8, 8, X)
                gs.append(gp)
            gh, gl = split(jnp.concatenate(gs, 0))
            ghs.append(gh)
            gls.append(gl)
        bacc[...] += z_forward(ghs, gls, ltf_ref, rk, yb * deep + y)
        gh = jnp.concatenate(ghs, 1)
        gl = jnp.concatenate(gls, 1)
        both = dot_nt(jnp.concatenate([xh, xl], 0), gh)
        lacc[...] += both[:256] + both[256:] + dot_nt(xh, gl)
        return carry

    lax.fori_loop(0, deep, step, 0, unroll=True)

    @pl.when(yb == pl.num_programs(0) - 1)
    def _():
        to_modes(rk, xt_ref, yf_ref, ph_ref, v_ref)
        same = iota((256, 256), 0) % 8 == iota((256, 256), 1) % 8
        rest = jnp.where(same, lacc[...], 0.0).reshape(C, 8, 256).sum(axis=1)
        pick = (iota((256, X), 0) // 8 == iota((256, X), 1)).astype(F32).astype(BF16)
        loc = jnp.zeros((C, X), F32)
        for _ in range(3):
            part = rest.astype(BF16)
            loc = loc + dot(part, pick)
            rest = rest - part.astype(F32)
        b = bacc[...]
        col = jnp.concatenate(
            [jnp.sum(b[:, g * X : (g + 1) * X], axis=1, keepdims=True) for g in range(4)], 0
        )
        diag = iota((C, X), 0) + C == iota((C, X), 1)
        row = jnp.sum(jnp.where(diag, col, 0.0), axis=0, keepdims=True)
        loc = loc + row
        loc = jnp.concatenate([loc[g * 8 : (g + 1) * 8] for g in range(4)], 1)
        extra = v_ref.shape[1] - 8
        for d in range(v_ref.shape[0]):
            v_ref[d, extra:, :] = loc


def back_kernel(
    gp_ref, m_ref, w_ref, lti_ref, xt_ref, yi_ref, ph_ref, *refs
):
    out_ref, qs, ws, gps, gp_sem = refs[-5:]
    yb = pl.program_id(0)
    gp = Rows(gp_ref, 0, gps, gp_sem)
    deep = gp.deep

    @pl.when(yb == 0)
    def _():
        gp.start()
        from_modes(m_ref, xt_ref, yi_ref, ph_ref, None, qs)
        weight_stack(w_ref, ws, dot)

    gp.copy(yb).wait()

    def step(y, carry):
        hl = [split(p) for p in load_parts(gps, yb * deep + y)]
        xh = jnp.concatenate([h for h, _ in hl], 1)
        xl = jnp.concatenate([l for _, l in hl], 1)
        conv = pointwise(ws, xh, xl)
        spec = dot(lti_ref[...], qs[yb * deep + y])
        for zo in range(4):
            for g in range(4):
                p = (
                    conv[g * 64 : (g + 1) * 64, zo * X : (zo + 1) * X]
                    + spec[zo * 64 : (zo + 1) * 64, g * X : (g + 1) * X]
                )
                out_ref[0, y, g * 8 : (g + 1) * 8, zo * 8 : (zo + 1) * 8, :] = p.reshape(8, 8, X)
        return carry

    lax.fori_loop(0, deep, step, 0, unroll=True)


def turn_kernel(w_ref, out_ref):
    for m in range(0, w_ref.shape[0], 2):
        four = jnp.concatenate([w_ref[m, 0], w_ref[m, 1], w_ref[m + 1, 0], w_ref[m + 1, 1]], 1)
        out_ref[m : m + 2] = four.T.reshape(2, 2, C, CQ)


def own_lanes(rows):
    return iota((rows, X), 0) % 8 == iota((rows, X), 1) // MY


def lane_period():
    return (iota((2 * X, X), 0) % MY == iota((2 * X, X), 1) % MY).astype(F32).astype(BF16)


def rows_table(r):
    a = np.einsum("gh,rs->grsh", np.eye(4), np.eye(r))
    a = np.repeat(a[..., None], 8, axis=-1).reshape(4 * r, r * C)
    return a.astype(ml_dtypes.bfloat16)


def total_of(ref):
    t = ref[0]
    for d in range(1, ref.shape[0]):
        t = t + ref[d]
    return t


def keep(side_ref, prev_ref, s):
    before = side_ref.shape[0] - s.shape[0]
    if prev_ref is not None:
        side_ref[:before, :] = prev_ref[...]
    side_ref[before:, :] = s


def mix_kernel(v_ref, wt_ref, sum_ref, *refs):
    mixed_ref, side_ref = refs[-2:]
    ml = wt_ref.shape[0]
    r = 2 * ml
    s = total_of(v_ref)
    keep(side_ref, refs[0] if len(refs) > 2 else None, s)

    folds = [None] * r
    for m in range(ml):
        re, im = s[m : m + 1], s[ml + m : ml + m + 1]
        wr, wi = wt_ref[m, 0], wt_ref[m, 1]
        for k, p in enumerate((re * wr - im * wi, re * wi + im * wr)):
            folds[k * ml + m] = (p[:, 0:128] + p[:, 128:256]) + (p[:, 256:384] + p[:, 384:512])
    v = jnp.concatenate(folds, 0)
    v = dot(jnp.concatenate(split(v), 1), lane_period())
    hi, lo = split(jnp.where(own_lanes(r * C), v, 0.0))
    v = dot(sum_ref[...], hi) + dot(sum_ref[...], lo)
    v = jnp.concatenate([v[g * r : (g + 1) * r] for g in range(4)], 1)
    for d in range(mixed_ref.shape[0]):
        mixed_ref[d] = v


def adjoint_kernel(v_ref, wt_ref, sum_ref, *refs):
    back_ref, side_ref = refs[-2:]
    ml = wt_ref.shape[0]
    r = 2 * ml
    s = total_of(v_ref)
    keep(side_ref, refs[0] if len(refs) > 2 else None, s)

    own = own_lanes(8)
    e = jnp.concatenate(
        [
            jnp.where(own, s[k : k + 1, g * X : (g + 1) * X], 0.0)
            for k in range(r)
            for g in range(4)
        ],
        0,
    )
    p = dot(jnp.concatenate(split(e), 1), lane_period())
    folds = [None] * r
    for m in range(ml):
        wr, wi = wt_ref[m, 0], wt_ref[m, 1]
        gr = jnp.concatenate([p[m * C : (m + 1) * C]] * 4, 1)
        gi = jnp.concatenate([p[(ml + m) * C : (ml + m + 1) * C]] * 4, 1)
        for k, v in enumerate((gr * wr + gi * wi, gi * wr - gr * wi)):
            folds[k * ml + m] = (v[0:8] + v[8:16]) + (v[16:24] + v[24:32])
    hi, lo = split(jnp.concatenate(folds, 0))
    ones = (iota((r, 8 * r), 0) == iota((r, 8 * r), 1) // 8).astype(F32).astype(BF16)
    v = dot(ones, hi) + dot(ones, lo)
    for d in range(back_ref.shape[0]):
        back_ref[d] = v


def weight_kernel(scaling, samples, *refs):
    gw_ref, local_ref, bias_ref, sides = refs[-4:]
    mb = gw_ref.shape[0]
    batches = sides.shape[0]
    rows = (sides.shape[1] // samples - 8) // 2
    ml = rows // 2

    @pl.when(pl.program_id(0) == 0)
    def _():
        for k in range(batches):
            at = lax.rem(lax.axis_index("batch") + batches - k, batches)
            sides[at] = refs[k][...]

    own = own_lanes(8)
    period = lane_period()
    pairs = [(s, b) for s in range(samples) for b in range(batches)]

    def spec_row(s, b, at):
        at = s * rows + at
        return sides[b, at : at + 1, :]

    def grad_row(s, b, at):
        at = samples * rows + s * (rows + 8) + at
        return sides[b, at : at + 1, :]

    def periodic(m):
        rows = [grad_row(s, b, at) for s, b in pairs for at in (m, ml + m)]
        e = jnp.concatenate(
            [jnp.where(own, r[:, g * X : (g + 1) * X], 0.0) for r in rows for g in range(4)], 0
        )
        return dot(jnp.concatenate(split(e), 1), period)

    def gradient(m):
        p = periodic(m)
        rr = [[None] * 4 for _ in range(2)]
        for k, (s, b) in enumerate(pairs):
            gr = p[2 * C * k : 2 * C * k + C]
            gi = p[2 * C * k + C : 2 * C * (k + 1)]
            ar, ai = spec_row(s, b, m), spec_row(s, b, ml + m)
            for g in range(4):
                cr, ci = ar[:, g * X : (g + 1) * X], ai[:, g * X : (g + 1) * X]
                for t, v in enumerate((cr * gr + ci * gi, cr * gi - ci * gr)):
                    rr[t][g] = v if rr[t][g] is None else rr[t][g] + v
        return [jnp.concatenate(r, 1) for r in rr]

    for c in range(ml // mb):

        @pl.when(pl.program_id(0) == c)
        def _():
            for k in range(0, mb, 2):
                m = c * mb + k
                v = jnp.concatenate(gradient(m) + gradient(m + 1), 0).T
                for t in range(4):
                    gw_ref[k + t // 2, t % 2] = v[:, t * C : (t + 1) * C]

    @pl.when(pl.program_id(0) == 0)
    def _():
        t = jnp.zeros((8, CQ), F32)
        for s, b in pairs:
            at = samples * rows + (s + 1) * (rows + 8)
            t = t + sides[b, at - 8 : at, :]
        t = jnp.concatenate([t[:, g * X : (g + 1) * X] for g in range(4)], 0) * scaling
        local_ref[...] = t[:, :C]
        bias_ref[...] = pltpu.roll(t, X - C, 1)[0:1, :C]


def whole(shape):
    return pl.BlockSpec(shape, lambda *_: (0,) * len(shape))


def params():
    return pltpu.CompilerParams(vmem_limit_bytes=VMEM_LIMIT)


def cost(flops, nbytes):
    return pl.CostEstimate(flops=int(flops), bytes_accessed=int(nbytes), transcendentals=0)


def shards(state_field, spectral_weight, local_weight, channel_bias, cotangent):
    samples, yl = state_field.shape[:2]
    pencils = lax.axis_size("pencil")
    batches = lax.axis_size("batch")
    ml = spectral_weight.shape[0]
    mg = max(ml, 8)
    groups = MODES // mg
    deep = math.gcd(YB, yl)
    yblocks = yl // deep
    n = yl * C
    rows = 2 * ml
    mb = math.gcd(4, ml)

    ltf = jnp.asarray(z_forward_table())
    lti = jnp.asarray(z_inverse_table())
    xt = jnp.asarray(x_table())
    yf, yi = (jnp.asarray(t) for t in y_tables(yl))
    phase = jnp.asarray(phase_table(yl, pencils))
    sums = jnp.asarray(rows_table(rows))
    bias = channel_bias.reshape(1, C)

    def pack(v):
        if mg == ml:
            return v
        extra = v[:, 2 * mg :]
        v = v[:, : 2 * mg].reshape(groups, 2, mg // ml, ml, CQ)
        v = v.transpose(0, 2, 1, 3, 4).reshape(pencils, rows, CQ)
        extra = jnp.broadcast_to(extra[:1], (pencils,) + extra.shape[1:])
        return jnp.concatenate([v, extra], axis=1)

    def unpack(v):
        if mg == ml:
            return v
        v = v.reshape(groups, mg // ml, 2, ml, CQ).transpose(0, 2, 1, 3, 4)
        return v.reshape(groups, 2 * mg, CQ)

    def exchange(v):
        return lax.all_to_all(v, "pencil", 0, 0, tiled=True)

    def around(v):
        return [v] + [
            lax.ppermute(v, "batch", [(i, (i + k) % batches) for i in range(batches)])
            for k in range(1, batches)
        ]

    def cells(s):
        return pl.BlockSpec((1, deep, C, Z, X), lambda yb: (s, yb, 0, 0, 0))

    held = [pltpu.VMEM((yl, C, Z, X), F32), pltpu.SemaphoreType.DMA((yblocks,))]

    any_space = pl.BlockSpec(memory_space=pl.ANY)
    cell_bytes = 4 * yl * C * Z * X
    table_bytes = 2 * (yf.size + yi.size + xt.size)
    field = jax.ShapeDtypeStruct(state_field.shape, F32)
    one_field = jax.ShapeDtypeStruct((1,) + state_field.shape[1:], F32)
    x_spec, yf_spec, yi_spec = whole(xt.shape), whole(yf.shape), whole(yi.shape)
    ph_spec = whole(phase.shape)
    rk = pltpu.VMEM((n, ZJ * X), F32)
    qs = pltpu.VMEM((yl, 3 * ZJP * 8, GX), BF16)
    ws = pltpu.VMEM((512, 256), BF16)

    def forward(s):
        return pl.pallas_call(
            functools.partial(forward_kernel, s),
            grid=(yblocks,),
            in_specs=[any_space, whole(ltf.shape), x_spec, yf_spec, ph_spec],
            out_specs=whole((groups, 2 * mg, CQ)),
            out_shape=jax.ShapeDtypeStruct((groups, 2 * mg, CQ), F32),
            scratch_shapes=[rk] + held,
            compiler_params=params(),
            cost_estimate=cost(2e9, cell_bytes + table_bytes),
            name="forward",
        )(state_field, ltf, xt, yf, phase)

    def middle(s, modes, prev):
        aliases = {} if prev is None else {11: 0}
        more = [] if prev is None else [prev]
        return pl.pallas_call(
            functools.partial(cell_kernel, s),
            grid=(yblocks,),
            in_specs=[
                any_space, any_space, whole((groups, 2 * mg, CQ)), whole((C, C)),
                whole((1, C)), whole(ltf.shape), whole(lti.shape),
                x_spec, yf_spec, yi_spec, ph_spec,
            ] + [any_space] * len(more),
            out_specs=[cells(s), cells(0), whole((groups, 2 * mg + 8, CQ))],
            out_shape=[field, one_field, jax.ShapeDtypeStruct((groups, 2 * mg + 8, CQ), F32)],
            scratch_shapes=[
                rk, qs, ws, pltpu.VMEM((256, 256), F32), pltpu.VMEM((8, GX), F32),
            ] + held + held,
            input_output_aliases=aliases,
            compiler_params=params(),
            cost_estimate=cost(16e9, 4 * cell_bytes + table_bytes),
            name="middle",
        )(state_field, cotangent, modes, local_weight, bias, ltf, lti, xt, yf, yi, phase, *more)

    def backward(s, gp, modes, prev):
        aliases = {} if prev is None else {7: 0}
        more = [] if prev is None else [prev]
        return pl.pallas_call(
            back_kernel,
            grid=(yblocks,),
            in_specs=[
                any_space, whole((groups, 2 * mg, CQ)), whole((C, C)), whole(lti.shape),
                x_spec, yi_spec, ph_spec,
            ] + [any_space] * len(more),
            out_specs=cells(s),
            out_shape=field,
            scratch_shapes=[qs, ws] + held,
            input_output_aliases=aliases,
            compiler_params=params(),
            cost_estimate=cost(6e9, 2 * cell_bytes + table_bytes),
            name="backward",
        )(gp, modes, local_weight, lti, xt, yi, phase, *more)

    def turned(w):
        return pl.pallas_call(
            turn_kernel,
            grid=(ml // mb,),
            in_specs=[pl.BlockSpec((mb, 2, CQ, C), lambda m: (m, 0, 0, 0))],
            out_specs=pl.BlockSpec((mb, 2, C, CQ), lambda m: (m, 0, 0, 0)),
            out_shape=jax.ShapeDtypeStruct((ml, 2, C, CQ), F32),
            compiler_params=params(),
            cost_estimate=cost(0, 5 * 4 * ml * 2 * CQ * C),
            name="turn",
        )(w.transpose(0, 1, 2, 4, 3).reshape(ml, 2, CQ, C))

    def mix(kernel, v, wt, prev, name):
        shape = (pencils, rows, CQ)
        side = (v.shape[1] + (0 if prev is None else prev.shape[0]), CQ)
        args = [v, wt, sums] if prev is None else [v, wt, sums, prev]
        return pl.pallas_call(
            kernel,
            grid=(1,),
            in_specs=[whole(a.shape) for a in args],
            out_specs=[whole(shape), whole(side)],
            out_shape=[jax.ShapeDtypeStruct(shape, F32), jax.ShapeDtypeStruct(side, F32)],
            compiler_params=params(),
            cost_estimate=cost(2e8, 4 * (wt.size + 2 * v.size)),
            name=name,
        )(*args)

    def weight_gradient(sides, after):
        scaling = 1.0 / math.sqrt(samples * batches * X * Y * Z)
        gw, local, b = pl.pallas_call(
            lambda *refs: weight_kernel(scaling, samples, *refs),
            grid=(ml // mb,),
            in_specs=[whole(a.shape) for a in sides] + [any_space],
            out_specs=[
                pl.BlockSpec((mb, 2, CQ, C), lambda m: (m, 0, 0, 0)),
                whole((C, C)),
                whole((1, C)),
            ],
            out_shape=[
                jax.ShapeDtypeStruct((ml, 2, CQ, C), F32),
                jax.ShapeDtypeStruct((C, C), F32),
                jax.ShapeDtypeStruct((1, C), F32),
            ],
            scratch_shapes=[pltpu.VMEM((batches,) + sides[0].shape, F32)],
            compiler_params=params(),
            cost_estimate=cost(2e8, 4 * 4 * ml * 2 * CQ * C),
            name="weight",
        )(*sides, after)
        gw = gw.reshape(ml, 2, C, MY, C).transpose(0, 1, 2, 4, 3)
        return gw, local, b.reshape(C)

    every = range(samples)
    sent = [exchange(pack(forward(s))) for s in every]
    wt = turned(spectral_weight)
    modes, side = [], None
    for s in every:
        mixed, side = mix(mix_kernel, sent[s], wt, side, "mix")
        modes.append(unpack(exchange(mixed)))

    layer_out = None
    gps, backs = [], []
    for s in every:
        layer_out, gp, v = middle(s, modes[s], layer_out)
        gps.append(gp)
        b, side = mix(adjoint_kernel, exchange(pack(v)), wt, side, "adjoint")
        backs.append(unpack(exchange(b)))
    sides = around(side)
    grad_state = None
    for s in every:
        grad_state = backward(s, gps[s], backs[s], grad_state)
    gw, local, b = weight_gradient(sides, grad_state)
    return (layer_out, grad_state, gw, local, b)


def solution(mesh):
    return jax.shard_map(
        shards,
        mesh=mesh,
        in_specs=(
            P("batch", "pencil", None, None, None),
            P("pencil", None, None, None, None),
            P(),
            P(),
            P("batch", "pencil", None, None, None),
        ),
        out_specs=(
            P("batch", "pencil", None, None, None),
            P("batch", "pencil", None, None, None),
            P("pencil", None, None, None, None),
            P(),
            P(),
        ),
        check_vma=False,
    )
```

```python
import functools
import math

import jax
import jax.numpy as jnp
import ml_dtypes
import numpy as np
from jax import lax
from jax.experimental import pallas as pl
from jax.experimental.pallas import tpu as pltpu
from jax.sharding import PartitionSpec as P

X = 128
Y = 128
Z = 32
C = 32
MX = 16
MY = 16
MZ = 8
MODES = MX * MZ
CQ = C * MY
ZJ = 9
ZJP = 10
GX = 4 * X
YB = 2

F32 = jnp.float32
BF16 = jnp.bfloat16
gelu_scale = math.sqrt(2.0 / math.pi)
cubic_term = 0.044715
VMEM_LIMIT = 56 * 1024 * 1024


def np_split(a):
    a = np.asarray(a, np.float32)
    hi = a.astype(ml_dtypes.bfloat16)
    lo = (a - hi.astype(np.float32)).astype(ml_dtypes.bfloat16)
    return hi, lo


def freqs(kept):
    return np.array([j if j < kept // 2 else j - kept for j in range(kept)])


def z_functions():
    z = np.arange(Z)
    rows = [np.cos(2 * np.pi * (j * z % Z) / Z) for j in range(5)]
    rows += [np.sin(2 * np.pi * (j * z % Z) / Z) for j in range(1, 5)]
    rows += [np.ones(Z)]
    return np.stack(rows)


def z_forward_table():
    zt = z_functions().reshape(ZJP, 4, 8)
    t = np.einsum("jab,cd->jcadb", zt, np.eye(8)).reshape(ZJP * 8, 256)
    hi, lo = np_split(t)
    return np.concatenate([hi, lo], 0)


def z_inverse_table():
    zt = z_functions().reshape(ZJP, 4, 8)
    t = np.einsum("jab,cd->acbjd", zt, np.eye(8)).reshape(256, ZJP * 8)
    hi, lo = np_split(t)
    return np.concatenate([hi, hi, lo], 1)


def x_table():
    x = np.arange(X)
    t = np.zeros((2, MX, MZ, ZJ, X))
    for a, fx in enumerate(freqs(MX)):
        cx = np.cos(2 * np.pi * (fx * x % X) / X)
        sx = np.sin(2 * np.pi * (fx * x % X) / X)
        for b, fz in enumerate(freqs(MZ)):
            k = abs(fz)
            t[0, a, b, k] = cx
            t[1, a, b, k] = sx
            if k > 0:
                t[0, a, b, 4 + k] = -np.sign(fz) * sx
                t[1, a, b, 4 + k] = np.sign(fz) * cx
    t = t.reshape(2 * MODES, ZJ * X) / math.sqrt(X * Y * Z)
    hi, lo = np_split(t)
    return np.concatenate([hi, lo], 0)


def channel_group(yl):
    return min(C, max(8, X // yl))


def y_tables(yl):
    cg = channel_group(yl)
    f = freqs(MY)
    ang = 2 * np.pi * (np.arange(yl)[:, None] * f[None, :] % Y) / Y
    t = np.stack([np.cos(ang), np.sin(ang)])
    fwd = np.einsum("tyq,cd->yctdq", t, np.eye(cg)).reshape(yl * cg, 2 * cg * MY)
    inv = np.einsum("tyq,cd->dqtyc", t, np.eye(cg)).reshape(cg * MY, 2 * yl * cg)
    out = []
    for m in (fwd, inv):
        hi, lo = np_split(m)
        out.append(np.concatenate([hi, hi, lo], 0))
    return out


def cell_row(yl, y, g):
    cg = channel_group(yl)
    return (g * 8 // cg) * (yl * cg) + y * cg + g * 8 % cg


def phase_table(yl, pencils):
    f = freqs(MY)
    ang = 2 * np.pi * (np.arange(pencils)[:, None] * yl * f[None, :] % Y) / Y
    t = np.stack([np.cos(ang), np.sin(ang)], 1)
    t = np.tile(t, (1, 4, C))
    return t.astype(np.float32)


def split(v):
    hi = v.astype(BF16)
    lo = (v - hi.astype(F32)).astype(BF16)
    return hi, lo


def dot(a, b):
    return lax.dot_general(a, b, (((1,), (0,)), ((), ())), preferred_element_type=F32)


def dot_nt(a, b):
    return lax.dot_general(a, b, (((1,), (1,)), ((), ())), preferred_element_type=F32)


def dot3(a, bh, bl, f=dot):
    ah, al = split(a)
    return f(ah, bh) + f(al, bh) + f(ah, bl)


def iota(shape, dim):
    return lax.broadcasted_iota(jnp.int32, shape, dim)


def regroup(parts):
    return jnp.concatenate(
        [jnp.concatenate([p[g * 64 : (g + 1) * 64] for p in parts], 0) for g in range(4)], 1
    )


def load_parts(ref, y):
    return [ref[y, :, zo * 8 : (zo + 1) * 8, :].reshape(256, X) for zo in range(4)]


class Rows:
    def __init__(self, source, sample, held, sems):
        self.source, self.sample, self.held, self.sems = source, sample, held, sems
        self.blocks = sems.shape[0]
        self.deep = held.shape[0] // self.blocks

    def copy(self, block):
        rows = pl.ds(block * self.deep, self.deep)
        return pltpu.make_async_copy(
            self.source.at[self.sample, rows], self.held.at[rows], self.sems.at[block]
        )

    def start(self):
        for block in range(self.blocks):
            self.copy(block).start()


def z_forward(his, los, ltf_ref, rk, y):
    gh, gl = regroup(his), regroup(los)
    n = ZJP * 8
    yl = rk.shape[0] // C
    both = dot(ltf_ref[...], gh)
    r = both[:n] + both[n:] + dot(ltf_ref[:n, :], gl)
    for g in range(4):
        rows = pl.ds(pl.multiple_of(cell_row(yl, y, g), 8), 8)
        for j in range(ZJ):
            rk[rows, j * X : (j + 1) * X] = r[j * 8 : (j + 1) * 8, g * X : (g + 1) * X]
    return r[ZJ * 8 :]


def by_group(v, table_ref, group):
    rows, lanes = v.shape
    parts = lanes // group
    v = jnp.concatenate([v[:, k * group : (k + 1) * group] for k in range(parts)], 0)
    hi, lo = split(v)
    r = dot(jnp.concatenate([hi, lo], 1), table_ref[: 2 * group, :])
    r = r + dot(hi, table_ref[2 * group :, :])
    half = r.shape[1] // 2
    return [
        jnp.concatenate(
            [r[k * rows : (k + 1) * rows, t * half : (t + 1) * half] for k in range(parts)], 1
        )
        for t in range(2)
    ]


def to_modes(rk, xt_ref, yf_ref, ph_ref, out_ref):
    rh, rl = split(rk[...])
    both = dot_nt(xt_ref[...], rh)
    n = 2 * MODES
    ab = both[:n] + both[n:] + dot_nt(xt_ref[:n, :], rl)
    zc, zs = by_group(ab, yf_ref, yf_ref.shape[0] // 3)
    re = zc[:MODES] - zs[MODES:]
    im = -(zc[MODES:] + zs[:MODES])
    pc, ps = own_phase(ph_ref)
    groups = out_ref.shape[0]
    mg = MODES // groups
    out_ref[:, :mg, :] = (re * pc + im * ps).reshape(groups, mg, CQ)
    out_ref[:, mg : 2 * mg, :] = (im * pc - re * ps).reshape(groups, mg, CQ)


def from_modes(m_ref, xt_ref, yi_ref, ph_ref, bias_ref, qs):
    groups, rows, _ = m_ref.shape
    mg = rows // 2
    re0 = m_ref[:, :mg, :].reshape(MODES, CQ)
    im0 = m_ref[:, mg:, :].reshape(MODES, CQ)
    pc, ps = own_phase(ph_ref)
    m = jnp.concatenate([re0 * pc - im0 * ps, im0 * pc + re0 * ps], 0)
    zc, zs = by_group(m, yi_ref, yi_ref.shape[0] // 3)
    re = zc[:MODES] - zs[MODES:]
    im = zc[MODES:] + zs[:MODES]
    yt = jnp.concatenate([re, -im], 0).T
    q = dot3(yt, xt_ref[: 2 * MODES, :], xt_ref[2 * MODES :, :])
    n = ZJP * 8
    yl = qs.shape[0]
    for y in range(yl):
        pieces = []
        for j in range(ZJ):
            pieces.append(
                jnp.concatenate(
                    [
                        q[cell_row(yl, y, g) : cell_row(yl, y, g) + 8, j * X : (j + 1) * X]
                        for g in range(4)
                    ],
                    1,
                )
            )
        if bias_ref is None:
            pieces.append(jnp.zeros((8, GX), F32))
        else:
            pieces.append(bias_rows(bias_ref))
        hi, lo = split(jnp.concatenate(pieces, 0))
        qs[y, 0:n, :] = hi
        qs[y, n : 2 * n, :] = lo
        qs[y, 2 * n :, :] = hi


def weight_stack(w_ref, ws, f):
    spread = (iota((256, C), 0) // 8 == iota((256, C), 1)).astype(F32).astype(BF16)
    same = iota((256, 256), 0) % 8 == iota((256, 256), 1) % 8

    def wide(part):
        t = dot_nt(f(spread, part).astype(BF16), spread)
        return jnp.where(same, t, 0.0).astype(BF16)

    hi, lo = split(w_ref[...])
    ws[0:256, :] = wide(hi)
    ws[256:512, :] = wide(lo)


def pointwise(ws, xh, xl):
    both = dot(ws[...], xh)
    return both[:256] + both[256:] + dot(ws[0:256, :], xl)


def bias_rows(b_ref):
    diag = iota((C, C), 0) == iota((C, C), 1)
    col = jnp.sum(jnp.where(diag, b_ref[...], 0.0), axis=1, keepdims=True)
    return jnp.concatenate(
        [jnp.broadcast_to(col[g * 8 : (g + 1) * 8], (8, X)) for g in range(4)], 1
    )


def own_phase(ph_ref):
    own = ph_ref[lax.axis_index("pencil")]
    return own[0:1], own[1:2]


def forward_kernel(s, x_ref, ltf_ref, xt_ref, yf_ref, ph_ref, out_ref, rk, xs, x_sem):
    yb = pl.program_id(0)
    x = Rows(x_ref, s, xs, x_sem)
    deep = x.deep

    @pl.when(yb == 0)
    def _():
        x.start()

    x.copy(yb).wait()

    def step(y, carry):
        hl = [split(p) for p in load_parts(xs, yb * deep + y)]
        z_forward([h for h, _ in hl], [l for _, l in hl], ltf_ref, rk, yb * deep + y)
        return carry

    lax.fori_loop(0, deep, step, 0, unroll=True)

    @pl.when(yb == pl.num_programs(0) - 1)
    def _():
        to_modes(rk, xt_ref, yf_ref, ph_ref, out_ref)


def cell_kernel(
    s, x_ref, ct_ref, m_ref, w_ref, bias_ref, ltf_ref, lti_ref, xt_ref, yf_ref, yi_ref, ph_ref,
    *refs,
):
    out_ref, gp_ref, v_ref, rk, qs, ws, lacc, bacc, xs, x_sem, cts, ct_sem = refs[-12:]
    yb = pl.program_id(0)
    x = Rows(x_ref, s, xs, x_sem)
    ct = Rows(ct_ref, s, cts, ct_sem)
    deep = x.deep

    @pl.when(yb == 0)
    def _():
        x.start()
        ct.start()
        from_modes(m_ref, xt_ref, yi_ref, ph_ref, bias_ref, qs)
        weight_stack(w_ref, ws, dot_nt)
        lacc[...] = jnp.zeros_like(lacc)
        bacc[...] = jnp.zeros_like(bacc)

    x.copy(yb).wait()
    ct.copy(yb).wait()

    def step(y, carry):
        hl = [split(p) for p in load_parts(xs, yb * deep + y)]
        xh = jnp.concatenate([h for h, _ in hl], 1)
        xl = jnp.concatenate([l for _, l in hl], 1)
        conv = pointwise(ws, xh, xl)
        spec = dot(lti_ref[...], qs[yb * deep + y])
        ghs, gls = [], []
        for zo in range(4):
            gs = []
            for g in range(4):
                p = (
                    conv[g * 64 : (g + 1) * 64, zo * X : (zo + 1) * X]
                    + spec[zo * 64 : (zo + 1) * 64, g * X : (g + 1) * X]
                )
                p2 = p * p
                u = p2 * (gelu_scale * cubic_term) + gelu_scale
                t = jnp.tanh(p * u)
                h = 0.5 * t + 0.5
                o = p * h
                d = p2 * (1.5 * gelu_scale * cubic_term) + 0.5 * gelu_scale
                slope = h + p * (1.0 - t * t) * d
                where = (0, y, slice(g * 8, (g + 1) * 8), slice(zo * 8, (zo + 1) * 8))
                out_ref[where] = o.reshape(8, 8, X)
                gp = cts[(yb * deep + y,) + where[2:]].reshape(64, X) * slope
                gp_ref[where] = gp.reshape(8, 8, X)
                gs.append(gp)
            gh, gl = split(jnp.concatenate(gs, 0))
            ghs.append(gh)
            gls.append(gl)
        bacc[...] += z_forward(ghs, gls, ltf_ref, rk, yb * deep + y)
        gh = jnp.concatenate(ghs, 1)
        gl = jnp.concatenate(gls, 1)
        both = dot_nt(jnp.concatenate([xh, xl], 0), gh)
        lacc[...] += both[:256] + both[256:] + dot_nt(xh, gl)
        return carry

    lax.fori_loop(0, deep, step, 0, unroll=True)

    @pl.when(yb == pl.num_programs(0) - 1)
    def _():
        to_modes(rk, xt_ref, yf_ref, ph_ref, v_ref)
        same = iota((256, 256), 0) % 8 == iota((256, 256), 1) % 8
        rest = jnp.where(same, lacc[...], 0.0).reshape(C, 8, 256).sum(axis=1)
        pick = (iota((256, X), 0) // 8 == iota((256, X), 1)).astype(F32).astype(BF16)
        loc = jnp.zeros((C, X), F32)
        for _ in range(3):
            part = rest.astype(BF16)
            loc = loc + dot(part, pick)
            rest = rest - part.astype(F32)
        b = bacc[...]
        col = jnp.concatenate(
            [jnp.sum(b[:, g * X : (g + 1) * X], axis=1, keepdims=True) for g in range(4)], 0
        )
        diag = iota((C, X), 0) + C == iota((C, X), 1)
        row = jnp.sum(jnp.where(diag, col, 0.0), axis=0, keepdims=True)
        loc = loc + row
        loc = jnp.concatenate([loc[g * 8 : (g + 1) * 8] for g in range(4)], 1)
        extra = v_ref.shape[1] - 8
        for d in range(v_ref.shape[0]):
            v_ref[d, extra:, :] = loc


def back_kernel(
    gp_ref, m_ref, w_ref, lti_ref, xt_ref, yi_ref, ph_ref, *refs
):
    out_ref, qs, ws, gps, gp_sem = refs[-5:]
    yb = pl.program_id(0)
    gp = Rows(gp_ref, 0, gps, gp_sem)
    deep = gp.deep

    @pl.when(yb == 0)
    def _():
        gp.start()
        from_modes(m_ref, xt_ref, yi_ref, ph_ref, None, qs)
        weight_stack(w_ref, ws, dot)

    gp.copy(yb).wait()

    def step(y, carry):
        hl = [split(p) for p in load_parts(gps, yb * deep + y)]
        xh = jnp.concatenate([h for h, _ in hl], 1)
        xl = jnp.concatenate([l for _, l in hl], 1)
        conv = pointwise(ws, xh, xl)
        spec = dot(lti_ref[...], qs[yb * deep + y])
        for zo in range(4):
            for g in range(4):
                p = (
                    conv[g * 64 : (g + 1) * 64, zo * X : (zo + 1) * X]
                    + spec[zo * 64 : (zo + 1) * 64, g * X : (g + 1) * X]
                )
                out_ref[0, y, g * 8 : (g + 1) * 8, zo * 8 : (zo + 1) * 8, :] = p.reshape(8, 8, X)
        return carry

    lax.fori_loop(0, deep, step, 0, unroll=True)


def turn_kernel(w_ref, out_ref):
    for m in range(0, w_ref.shape[0], 2):
        four = jnp.concatenate([w_ref[m, 0], w_ref[m, 1], w_ref[m + 1, 0], w_ref[m + 1, 1]], 1)
        out_ref[m : m + 2] = four.T.reshape(2, 2, C, CQ)


def own_lanes(rows):
    return iota((rows, X), 0) % 8 == iota((rows, X), 1) // MY


def lane_period():
    return (iota((2 * X, X), 0) % MY == iota((2 * X, X), 1) % MY).astype(F32).astype(BF16)


def rows_table(r):
    a = np.einsum("gh,rs->grsh", np.eye(4), np.eye(r))
    a = np.repeat(a[..., None], 8, axis=-1).reshape(4 * r, r * C)
    return a.astype(ml_dtypes.bfloat16)


def total_of(ref):
    t = ref[0]
    for d in range(1, ref.shape[0]):
        t = t + ref[d]
    return t


def keep(side_ref, prev_ref, s):
    before = side_ref.shape[0] - s.shape[0]
    if prev_ref is not None:
        side_ref[:before, :] = prev_ref[...]
    side_ref[before:, :] = s


def mix_kernel(v_ref, wt_ref, sum_ref, *refs):
    mixed_ref, side_ref = refs[-2:]
    ml = wt_ref.shape[0]
    r = 2 * ml
    s = total_of(v_ref)
    keep(side_ref, refs[0] if len(refs) > 2 else None, s)

    folds = [None] * r
    for m in range(ml):
        re, im = s[m : m + 1], s[ml + m : ml + m + 1]
        wr, wi = wt_ref[m, 0], wt_ref[m, 1]
        for k, p in enumerate((re * wr - im * wi, re * wi + im * wr)):
            folds[k * ml + m] = (p[:, 0:128] + p[:, 128:256]) + (p[:, 256:384] + p[:, 384:512])
    v = jnp.concatenate(folds, 0)
    v = dot(jnp.concatenate(split(v), 1), lane_period())
    hi, lo = split(jnp.where(own_lanes(r * C), v, 0.0))
    v = dot(sum_ref[...], hi) + dot(sum_ref[...], lo)
    v = jnp.concatenate([v[g * r : (g + 1) * r] for g in range(4)], 1)
    for d in range(mixed_ref.shape[0]):
        mixed_ref[d] = v


def adjoint_kernel(v_ref, wt_ref, sum_ref, *refs):
    back_ref, side_ref = refs[-2:]
    ml = wt_ref.shape[0]
    r = 2 * ml
    s = total_of(v_ref)
    keep(side_ref, refs[0] if len(refs) > 2 else None, s)

    own = own_lanes(8)
    e = jnp.concatenate(
        [
            jnp.where(own, s[k : k + 1, g * X : (g + 1) * X], 0.0)
            for k in range(r)
            for g in range(4)
        ],
        0,
    )
    p = dot(jnp.concatenate(split(e), 1), lane_period())
    folds = [None] * r
    for m in range(ml):
        wr, wi = wt_ref[m, 0], wt_ref[m, 1]
        gr = jnp.concatenate([p[m * C : (m + 1) * C]] * 4, 1)
        gi = jnp.concatenate([p[(ml + m) * C : (ml + m + 1) * C]] * 4, 1)
        for k, v in enumerate((gr * wr + gi * wi, gi * wr - gr * wi)):
            folds[k * ml + m] = (v[0:8] + v[8:16]) + (v[16:24] + v[24:32])
    hi, lo = split(jnp.concatenate(folds, 0))
    ones = (iota((r, 8 * r), 0) == iota((r, 8 * r), 1) // 8).astype(F32).astype(BF16)
    v = dot(ones, hi) + dot(ones, lo)
    for d in range(back_ref.shape[0]):
        back_ref[d] = v


def weight_kernel(scaling, samples, *refs):
    gw_ref, local_ref, bias_ref, sides = refs[-4:]
    mb = gw_ref.shape[0]
    batches = sides.shape[0]
    rows = (sides.shape[1] // samples - 8) // 2
    ml = rows // 2

    @pl.when(pl.program_id(0) == 0)
    def _():
        for k in range(batches):
            at = lax.rem(lax.axis_index("batch") + batches - k, batches)
            sides[at] = refs[k][...]

    own = own_lanes(8)
    period = lane_period()
    pairs = [(s, b) for s in range(samples) for b in range(batches)]

    def spec_row(s, b, at):
        at = s * rows + at
        return sides[b, at : at + 1, :]

    def grad_row(s, b, at):
        at = samples * rows + s * (rows + 8) + at
        return sides[b, at : at + 1, :]

    def periodic(m):
        rows = [grad_row(s, b, at) for s, b in pairs for at in (m, ml + m)]
        e = jnp.concatenate(
            [jnp.where(own, r[:, g * X : (g + 1) * X], 0.0) for r in rows for g in range(4)], 0
        )
        return dot(jnp.concatenate(split(e), 1), period)

    def gradient(m):
        p = periodic(m)
        rr = [[None] * 4 for _ in range(2)]
        for k, (s, b) in enumerate(pairs):
            gr = p[2 * C * k : 2 * C * k + C]
            gi = p[2 * C * k + C : 2 * C * (k + 1)]
            ar, ai = spec_row(s, b, m), spec_row(s, b, ml + m)
            for g in range(4):
                cr, ci = ar[:, g * X : (g + 1) * X], ai[:, g * X : (g + 1) * X]
                for t, v in enumerate((cr * gr + ci * gi, cr * gi - ci * gr)):
                    rr[t][g] = v if rr[t][g] is None else rr[t][g] + v
        return [jnp.concatenate(r, 1) for r in rr]

    for c in range(ml // mb):

        @pl.when(pl.program_id(0) == c)
        def _():
            for k in range(0, mb, 2):
                m = c * mb + k
                v = jnp.concatenate(gradient(m) + gradient(m + 1), 0).T
                for t in range(4):
                    gw_ref[k + t // 2, t % 2] = v[:, t * C : (t + 1) * C]

    @pl.when(pl.program_id(0) == 0)
    def _():
        t = jnp.zeros((8, CQ), F32)
        for s, b in pairs:
            at = samples * rows + (s + 1) * (rows + 8)
            t = t + sides[b, at - 8 : at, :]
        t = jnp.concatenate([t[:, g * X : (g + 1) * X] for g in range(4)], 0) * scaling
        local_ref[...] = t[:, :C]
        bias_ref[...] = pltpu.roll(t, X - C, 1)[0:1, :C]


def whole(shape):
    return pl.BlockSpec(shape, lambda *_: (0,) * len(shape))


def params():
    return pltpu.CompilerParams(vmem_limit_bytes=VMEM_LIMIT)


def cost(flops, nbytes):
    return pl.CostEstimate(flops=int(flops), bytes_accessed=int(nbytes), transcendentals=0)


def shards(state_field, spectral_weight, local_weight, channel_bias, cotangent):
    samples, yl = state_field.shape[:2]
    pencils = lax.axis_size("pencil")
    batches = lax.axis_size("batch")
    ml = spectral_weight.shape[0]
    mg = max(ml, 8)
    groups = MODES // mg
    deep = math.gcd(YB, yl)
    yblocks = yl // deep
    n = yl * C
    rows = 2 * ml
    mb = math.gcd(4, ml)

    ltf = jnp.asarray(z_forward_table())
    lti = jnp.asarray(z_inverse_table())
    xt = jnp.asarray(x_table())
    yf, yi = (jnp.asarray(t) for t in y_tables(yl))
    phase = jnp.asarray(phase_table(yl, pencils))
    sums = jnp.asarray(rows_table(rows))
    bias = channel_bias.reshape(1, C)

    def pack(v):
        if mg == ml:
            return v
        extra = v[:, 2 * mg :]
        v = v[:, : 2 * mg].reshape(groups, 2, mg // ml, ml, CQ)
        v = v.transpose(0, 2, 1, 3, 4).reshape(pencils, rows, CQ)
        extra = jnp.broadcast_to(extra[:1], (pencils,) + extra.shape[1:])
        return jnp.concatenate([v, extra], axis=1)

    def unpack(v):
        if mg == ml:
            return v
        v = v.reshape(groups, mg // ml, 2, ml, CQ).transpose(0, 2, 1, 3, 4)
        return v.reshape(groups, 2 * mg, CQ)

    def exchange(v):
        return lax.all_to_all(v, "pencil", 0, 0, tiled=True)

    def around(v):
        return [v] + [
            lax.ppermute(v, "batch", [(i, (i + k) % batches) for i in range(batches)])
            for k in range(1, batches)
        ]

    def cells(s):
        return pl.BlockSpec((1, deep, C, Z, X), lambda yb: (s, yb, 0, 0, 0))

    held = [pltpu.VMEM((yl, C, Z, X), F32), pltpu.SemaphoreType.DMA((yblocks,))]

    any_space = pl.BlockSpec(memory_space=pl.ANY)
    cell_bytes = 4 * yl * C * Z * X
    table_bytes = 2 * (yf.size + yi.size + xt.size)
    field = jax.ShapeDtypeStruct(state_field.shape, F32)
    one_field = jax.ShapeDtypeStruct((1,) + state_field.shape[1:], F32)
    x_spec, yf_spec, yi_spec = whole(xt.shape), whole(yf.shape), whole(yi.shape)
    ph_spec = whole(phase.shape)
    rk = pltpu.VMEM((n, ZJ * X), F32)
    qs = pltpu.VMEM((yl, 3 * ZJP * 8, GX), BF16)
    ws = pltpu.VMEM((512, 256), BF16)

    def forward(s):
        return pl.pallas_call(
            functools.partial(forward_kernel, s),
            grid=(yblocks,),
            in_specs=[any_space, whole(ltf.shape), x_spec, yf_spec, ph_spec],
            out_specs=whole((groups, 2 * mg, CQ)),
            out_shape=jax.ShapeDtypeStruct((groups, 2 * mg, CQ), F32),
            scratch_shapes=[rk] + held,
            compiler_params=params(),
            cost_estimate=cost(2e9, cell_bytes + table_bytes),
            name="forward",
        )(state_field, ltf, xt, yf, phase)

    def middle(s, modes, prev):
        aliases = {} if prev is None else {11: 0}
        more = [] if prev is None else [prev]
        return pl.pallas_call(
            functools.partial(cell_kernel, s),
            grid=(yblocks,),
            in_specs=[
                any_space, any_space, whole((groups, 2 * mg, CQ)), whole((C, C)),
                whole((1, C)), whole(ltf.shape), whole(lti.shape),
                x_spec, yf_spec, yi_spec, ph_spec,
            ] + [any_space] * len(more),
            out_specs=[cells(s), cells(0), whole((groups, 2 * mg + 8, CQ))],
            out_shape=[field, one_field, jax.ShapeDtypeStruct((groups, 2 * mg + 8, CQ), F32)],
            scratch_shapes=[
                rk, qs, ws, pltpu.VMEM((256, 256), F32), pltpu.VMEM((8, GX), F32),
            ] + held + held,
            input_output_aliases=aliases,
            compiler_params=params(),
            cost_estimate=cost(16e9, 4 * cell_bytes + table_bytes),
            name="middle",
        )(state_field, cotangent, modes, local_weight, bias, ltf, lti, xt, yf, yi, phase, *more)

    def backward(s, gp, modes, prev):
        aliases = {} if prev is None else {7: 0}
        more = [] if prev is None else [prev]
        return pl.pallas_call(
            back_kernel,
            grid=(yblocks,),
            in_specs=[
                any_space, whole((groups, 2 * mg, CQ)), whole((C, C)), whole(lti.shape),
                x_spec, yi_spec, ph_spec,
            ] + [any_space] * len(more),
            out_specs=cells(s),
            out_shape=field,
            scratch_shapes=[qs, ws] + held,
            input_output_aliases=aliases,
            compiler_params=params(),
            cost_estimate=cost(6e9, 2 * cell_bytes + table_bytes),
            name="backward",
        )(gp, modes, local_weight, lti, xt, yi, phase, *more)

    def turned(w):
        return pl.pallas_call(
            turn_kernel,
            grid=(ml // mb,),
            in_specs=[pl.BlockSpec((mb, 2, CQ, C), lambda m: (m, 0, 0, 0))],
            out_specs=pl.BlockSpec((mb, 2, C, CQ), lambda m: (m, 0, 0, 0)),
            out_shape=jax.ShapeDtypeStruct((ml, 2, C, CQ), F32),
            compiler_params=params(),
            cost_estimate=cost(0, 5 * 4 * ml * 2 * CQ * C),
            name="turn",
        )(w.transpose(0, 1, 2, 4, 3).reshape(ml, 2, CQ, C))

    def mix(kernel, v, wt, prev, name):
        shape = (pencils, rows, CQ)
        side = (v.shape[1] + (0 if prev is None else prev.shape[0]), CQ)
        args = [v, wt, sums] if prev is None else [v, wt, sums, prev]
        return pl.pallas_call(
            kernel,
            grid=(1,),
            in_specs=[whole(a.shape) for a in args],
            out_specs=[whole(shape), whole(side)],
            out_shape=[jax.ShapeDtypeStruct(shape, F32), jax.ShapeDtypeStruct(side, F32)],
            compiler_params=params(),
            cost_estimate=cost(2e8, 4 * (wt.size + 2 * v.size)),
            name=name,
        )(*args)

    def weight_gradient(sides, after):
        scaling = 1.0 / math.sqrt(samples * batches * X * Y * Z)
        gw, local, b = pl.pallas_call(
            lambda *refs: weight_kernel(scaling, samples, *refs),
            grid=(ml // mb,),
            in_specs=[whole(a.shape) for a in sides] + [any_space],
            out_specs=[
                pl.BlockSpec((mb, 2, CQ, C), lambda m: (m, 0, 0, 0)),
                whole((C, C)),
                whole((1, C)),
            ],
            out_shape=[
                jax.ShapeDtypeStruct((ml, 2, CQ, C), F32),
                jax.ShapeDtypeStruct((C, C), F32),
                jax.ShapeDtypeStruct((1, C), F32),
            ],
            scratch_shapes=[pltpu.VMEM((batches,) + sides[0].shape, F32)],
            compiler_params=params(),
            cost_estimate=cost(2e8, 4 * 4 * ml * 2 * CQ * C),
            name="weight",
        )(*sides, after)
        gw = gw.reshape(ml, 2, C, MY, C).transpose(0, 1, 2, 4, 3)
        return gw, local, b.reshape(C)

    every = range(samples)
    sent = [exchange(pack(forward(s))) for s in every]
    wt = turned(spectral_weight)
    modes, side = [], None
    for s in every:
        mixed, side = mix(mix_kernel, sent[s], wt, side, "mix")
        modes.append(unpack(exchange(mixed)))

    layer_out = None
    gps, backs = [], []
    for s in every:
        layer_out, gp, v = middle(s, modes[s], layer_out)
        gps.append(gp)
        b, side = mix(adjoint_kernel, exchange(pack(v)), wt, side, "adjoint")
        backs.append(unpack(exchange(b)))
    sides = around(side)
    grad_state = None
    for s in every:
        grad_state = backward(s, gps[s], backs[s], grad_state)
    gw, local, b = weight_gradient(sides, grad_state)
    return (layer_out, grad_state, gw, local, b)


def solution(mesh):
    return jax.shard_map(
        shards,
        mesh=mesh,
        in_specs=(
            P("batch", "pencil", None, None, None),
            P("pencil", None, None, None, None),
            P(),
            P(),
            P("batch", "pencil", None, None, None),
        ),
        out_specs=(
            P("batch", "pencil", None, None, None),
            P("batch", "pencil", None, None, None),
            P("pencil", None, None, None, None),
            P(),
            P(),
        ),
        check_vma=False,
    )
```
